128 devices in a mesh: rep: 4 (over z_lo, core), ctx: 16 (over x, y), tp: 2 (over z_hi).
Axes of the slice: x: 4, y: 4, z: 4 (z_hi: 2, z_lo: 2; z = z_hi * 2 + z_lo), core: 2. Of those that a mesh axis runs over, the one named last changes fastest.
Arguments:
- tokens: bfloat16 [8, 1024, 1024], P('rep', 'ctx'), may hold values from -6 to 6
- cotangent: bfloat16 [8, 1024, 1024], P('rep', 'ctx'), may hold values from -6 to 6
- segments: int32 [8, 1024], P('rep'), may hold values from 0 to 3, as said below
- w_query: bfloat16 [1, 1024, 2048], P(None, 'ctx', 'tp'), may hold values from -0.1875 to 0.1875
- w_key: bfloat16 [1, 1024, 1024], P(None, 'ctx', 'tp'), may hold values from -0.1875 to 0.1875
- w_value: bfloat16 [1, 1024, 1024], P(None, 'ctx', 'tp'), may hold values from -0.1875 to 0.1875
- w_output: bfloat16 [1, 2048, 1024], P(None, 'tp', 'ctx'), may hold values from -0.75 to 0.75
- w_gate: bfloat16 [1, 1024, 3072], P(None, 'ctx', 'tp'), may hold values from -0.1875 to 0.1875
- w_up: bfloat16 [1, 1024, 3072], P(None, 'ctx', 'tp'), may hold values from -0.1875 to 0.1875
- w_down: bfloat16 [1, 3072, 1024], P(None, 'tp', 'ctx'), may hold values from -0.109375 to 0.109375
- norm_attn: bfloat16 [1, 1024], P(None, 'ctx'), may hold values from 0.25 to 1.75
- norm_mlp: bfloat16 [1, 1024], P(None, 'ctx'), may hold values from 0.25 to 1.75
- norm_query: bfloat16 [1, 128], P(None, 'ctx'), may hold values from 0.25 to 1.75
- norm_key: bfloat16 [1, 128], P(None, 'ctx'), may hold values from 0.25 to 1.75
Outputs:
- out_tokens: float32 [8, 1024, 1024], P('rep', 'ctx')
- tokens_grad: float32 [8, 1024, 1024], P('rep', 'ctx')
- w_query_grad: float32 [1, 1024, 2048], P(None, 'ctx', 'tp')
- w_key_grad: float32 [1, 1024, 1024], P(None, 'ctx', 'tp')
- w_value_grad: float32 [1, 1024, 1024], P(None, 'ctx', 'tp')
- w_output_grad: float32 [1, 2048, 1024], P(None, 'tp', 'ctx')
- w_gate_grad: float32 [1, 1024, 3072], P(None, 'ctx', 'tp')
- w_up_grad: float32 [1, 1024, 3072], P(None, 'ctx', 'tp')
- w_down_grad: float32 [1, 3072, 1024], P(None, 'tp', 'ctx')
- norm_attn_grad: float32 [1, 1024], P(None, 'ctx')
- norm_mlp_grad: float32 [1, 1024], P(None, 'ctx')
- norm_query_grad: float32 [1, 128], P(None, 'ctx')
- norm_key_grad: float32 [1, 128], P(None, 'ctx')
The draws below stay inside these ranges and needn't reach their ends.
Inputs may be any that keep to these rules, and one draw needn't show every extreme that they name: `segments`: within each sequence the ids start at 0, never fall and rise by one at each new document; every document has 200 tokens or more. In each group of 2 consecutive sequences one sequence, drawn from the seed, is a single document and another holds four.
All inputs are finite; a program needn't handle non-finite values.
Results may differ from the reference program's by a relative error of at most 0.017.
Values may be sent and summed in bfloat16 or wider, within the bound.
No kernel may reach another device: no remote copies, remote signals or barrier semaphores. Data moves between devices by JAX's collectives and lax.ppermute only.
A program may use at most 128 MiB of HBM per device.

```python
import math
import jax
import jax.numpy as jnp
from jax import lax

D = 1024
H = 16
KVH = 8
HD = 128
FF = 3072
L = 1024
DOC_MIN = 200
LAYERS = 1
SEQS = 2
SEQS_ALL = 8
N_REP = 4


def draw_segments(key, part):
    key = jax.random.fold_in(key, 7)
    key_choose, key_count, key_cut = jax.random.split(key, 3)
    total_seqs = SEQS * N_REP
    group_pos = jnp.arange(total_seqs, dtype=jnp.int32) % SEQS
    chosen = jnp.repeat(jax.random.randint(key_choose, (N_REP,), 0, SEQS), SEQS)
    doc_count = jax.random.randint(key_count, (total_seqs,), 2, 5)
    doc_count = jnp.where(group_pos == chosen, 1, doc_count)
    doc_count = jnp.where(group_pos == (chosen + 1) % SEQS, 4, doc_count)
    spare = L - doc_count * DOC_MIN
    slot_index = jnp.arange(3, dtype=jnp.int32)
    used = slot_index[None, :] < doc_count[:, None] - 1
    cuts = jax.random.randint(key_cut, (total_seqs, 3), 0, spare[:, None] + 1)
    cuts = jnp.sort(jnp.where(used, cuts, spare[:, None]), axis=1)
    starts = jnp.where(used, (slot_index[None, :] + 1) * DOC_MIN + cuts, L)
    token_index = jnp.arange(L, dtype=jnp.int32)
    return jnp.sum((token_index[None, :, None] >= starts[:, None, :]).astype(jnp.int32), axis=2)


def block_levels(key, shape, cuts, smallest, top_value):
    def one(position, shards_of):
        heights = jax.random.uniform(jax.random.fold_in(jax.random.fold_in(key, 6), position), (shards_of,), jnp.float32, smallest / len(cuts), top_value / len(cuts))
        return jnp.repeat(jnp.exp(heights), shape[position] // shards_of).reshape((-1,) + (1,) * (len(shape) - position - 1))

    level = one(*cuts[0])
    for cut in cuts[1:]:
        level = level * one(*cut)
    return level


def normal_values(rng, extent, deviation, limit, pieces=(), kind=jnp.bfloat16):
    level = block_levels(rng, extent, pieces, -0.22, 0.18) if pieces else 1.0
    array = jax.random.normal(rng, extent, jnp.float32) * deviation * level
    return jnp.minimum(jnp.maximum(array, -limit), limit).astype(kind)


def setup_inputs(seed: int = 0) -> dict:
    splits = jax.random.split(jax.random.key(seed), 15)
    return {
        "tokens": normal_values(splits[0], (SEQS_ALL, L, D), 1.0, 6.0, ((0, 4), (1, 16))),
        "cotangent": normal_values(splits[1], (SEQS_ALL, L, D), 1.0, 6.0, ((0, 4), (1, 16))),
        "segments": draw_segments(jax.random.fold_in(splits[14], 71), 0),
        "w_query": normal_values(splits[3], (LAYERS, D, H * HD), D ** -0.5, 0.1875, ((1, 16), (2, 2))),
        "w_key": normal_values(splits[4], (LAYERS, D, KVH * HD), D ** -0.5, 0.1875, ((1, 16), (2, 2))),
        "w_value": normal_values(splits[5], (LAYERS, D, KVH * HD), D ** -0.5, 0.1875, ((1, 16), (2, 2))),
        "w_output": normal_values(splits[6], (LAYERS, H * HD, D), (HD // 2) ** -0.5, 0.75, ((1, 2), (2, 16))),
        "w_gate": normal_values(splits[7], (LAYERS, D, FF), D ** -0.5, 0.1875, ((1, 16), (2, 2))),
        "w_up": normal_values(splits[8], (LAYERS, D, FF), D ** -0.5, 0.1875, ((1, 16), (2, 2))),
        "w_down": normal_values(splits[9], (LAYERS, FF, D), FF ** -0.5, 0.109375, ((1, 2), (2, 16))),
        "norm_attn": jnp.clip(1.0 + 0.15 * jax.random.normal(splits[10], (LAYERS, D), jnp.float32), 0.25, 1.75).astype(jnp.bfloat16),
        "norm_mlp": jnp.clip(1.0 + 0.15 * jax.random.normal(splits[11], (LAYERS, D), jnp.float32), 0.25, 1.75).astype(jnp.bfloat16),
        "norm_query": jnp.clip(1.0 + 0.15 * jax.random.normal(splits[12], (LAYERS, HD), jnp.float32), 0.25, 1.75).astype(jnp.bfloat16),
        "norm_key": jnp.clip(1.0 + 0.15 * jax.random.normal(splits[13], (LAYERS, HD), jnp.float32), 0.25, 1.75).astype(jnp.bfloat16),
    }


norm_eps = 1e-06
rope_base = 1000000.0
masked_score = -1e+30

@jax.custom_vjp
def low(v):
    return lax.optimization_barrier(v.astype(jnp.bfloat16)).astype(jnp.float32)

@jax.custom_vjp
def low_back(v):
    return v

def low_keep(v):
    return (low(v), None)

def low_pass(kept, grad):
    return (grad,)

def back_keep(v):
    return (v, None)

def back_low(kept, grad):
    return (low(grad),)
low.defvjp(low_keep, low_pass)
low_back.defvjp(back_keep, back_low)

def positions(segments):
    length = segments.shape[-1]
    token_index = jnp.arange(length, dtype=jnp.int32)
    change = jnp.concatenate([jnp.ones(segments[:, :1].shape, jnp.int32), (segments[:, 1:] != segments[:, :-1]).astype(jnp.int32)], axis=1)
    starts = lax.cummax(jnp.where(change > 0, token_index[None, :], jnp.zeros((), jnp.int32)), axis=1)
    return token_index[None, :] - starts

def rope_tables(pos_table, head_size):
    half_size = head_size // 2
    freq_table = jnp.exp(jnp.arange(half_size, dtype=jnp.float32) * (-2.0 * math.log(rope_base) / head_size))
    angles = pos_table.astype(jnp.float32)[..., None] * freq_table
    angles = jnp.concatenate([angles, angles], -1)
    return (jnp.cos(angles), jnp.sin(angles))

def rms_norm(values):
    return values * lax.rsqrt(lax.optimization_barrier(jnp.mean(values * values, -1, keepdims=True)) + norm_eps)

def rotate(values, cosine, sine):
    half_size = values.shape[-1] // 2
    turned = jnp.concatenate([-values[..., half_size:], values[..., :half_size]], -1)
    return values * cosine + turned * sine

def matmul_high(left, right):
    return jnp.dot(left, right, precision=lax.Precision.HIGHEST)

def attend(block_item):
    queries, keys, values, seg_row = block_item
    length, head_count, head_size = queries.shape
    keyhead_count = keys.shape[1]
    grouped = queries.reshape(length, keyhead_count, head_count // keyhead_count, head_size)
    scores = jnp.einsum('qgrd,kgd->grqk', grouped, keys, precision=lax.Precision.HIGHEST) * (1.0 / math.sqrt(head_size))
    token_index = jnp.arange(length, dtype=jnp.int32)
    allowed = (seg_row[:, None] == seg_row[None, :]) & (token_index[None, :] <= token_index[:, None])
    scores = jnp.where(allowed[None, None], low_back(scores), masked_score)
    row_max = lax.optimization_barrier(jnp.max(scores, -1, keepdims=True))
    weights_exp = jnp.exp(scores - row_max)
    probs = weights_exp / lax.optimization_barrier(jnp.sum(weights_exp, -1, keepdims=True))
    mixed = jnp.einsum('grqk,kgd->qgrd', low(probs), values, precision=lax.Precision.HIGHEST)
    return mixed.reshape(length, head_count * head_size)

def layer_forward(hidden, weights, seg_group, cosine, sine):
    query_w, key_w, value_w, out_w, gate_w, up_w, down_w, attn_gain, mlp_gain, qnorm_gain, knorm_gain = weights
    count, length, width = hidden.shape
    flat = hidden.reshape(count * length, width)
    attn_in = low(rms_norm(flat) * attn_gain)
    query_raw = low_back(matmul_high(attn_in, query_w)).reshape(count, length, -1, HD)
    key_raw = low_back(matmul_high(attn_in, key_w)).reshape(count, length, -1, HD)
    value = low(low_back(matmul_high(attn_in, value_w))).reshape(count, length, -1, HD)
    cos_heads = cosine[:, :, None, :]
    sin_heads = sine[:, :, None, :]
    queries = low(rotate(rms_norm(query_raw) * qnorm_gain, cos_heads, sin_heads))
    keys = low(rotate(rms_norm(key_raw) * knorm_gain, cos_heads, sin_heads))
    mixed = lax.map(jax.checkpoint(attend), (queries, keys, value, seg_group))
    mixed = low(mixed.reshape(count * length, -1))
    hidden_mid = flat + low_back(matmul_high(mixed, out_w))
    mlp_in = low(rms_norm(hidden_mid) * mlp_gain)
    gate_pre = low_back(matmul_high(mlp_in, gate_w))
    up_pre = low_back(matmul_high(mlp_in, up_w))
    act = low(jax.nn.silu(gate_pre) * up_pre)
    hidden_out = hidden_mid + low_back(matmul_high(act, down_w))
    return hidden_out.reshape(count, length, width)

def reference(tokens, cotangent, segments, w_query, w_key, w_value, w_output, w_gate, w_up, w_down, norm_attn, norm_mlp, norm_query, norm_key):
    params = tuple((w.astype(jnp.float32) for w in (w_query, w_key, w_value, w_output, w_gate, w_up, w_down, norm_attn, norm_mlp, norm_query, norm_key)))
    total_seqs = segments.shape[0]
    group_size = math.gcd(total_seqs, 4)
    step_count = total_seqs // group_size
    cosine, sine = rope_tables(positions(segments), HD)

    def regroup(values):
        return values.reshape((step_count, group_size) + values.shape[1:])
    items = (regroup(tokens.astype(jnp.float32)), regroup(cotangent.astype(jnp.float32)), regroup(segments), regroup(cosine), regroup(sine))

    def step_fn(totals, block_item):
        x_group, cot_group, seg_group, cos_group, sin_group = block_item

        def forward(x_in, param_set):
            hidden = x_in
            for layer_idx in range(LAYERS):
                hidden = layer_forward(hidden, tuple((w[layer_idx] for w in param_set)), seg_group, cos_group, sin_group)
            return hidden
        result, pull_back = jax.vjp(forward, x_group, params)
        input_grad, param_grads = pull_back(cot_group)
        return (tuple((a + b for a, b in zip(totals, param_grads))), (result, input_grad))
    zero_grads = tuple((jnp.zeros(w.shape, jnp.float32) for w in params))
    grads, (results, input_grads) = lax.scan(step_fn, zero_grads, items)
    shape = tokens.shape
    return (results.reshape(shape), input_grads.reshape(shape), grads[0], grads[1], grads[2], grads[3], grads[4], grads[5], grads[6], grads[7], grads[8], grads[9], grads[10])
```

```python
import math

import jax
import jax.numpy as jnp
from jax import lax
from jax.sharding import PartitionSpec as P

HD = 128
D = 1024
SCALE = 1.0 / math.sqrt(HD)
norm_eps = 1e-06
rope_base = 1000000.0
masked_score = -1e30
bf16 = jnp.bfloat16
f32 = jnp.float32


def core_swap(values):
    return lax.ppermute(values, "rep", [(0, 1), (1, 0), (2, 3), (3, 2)])


def zlo_swap(values):
    return lax.ppermute(values, "rep", [(0, 2), (1, 3), (2, 0), (3, 1)])


def tp_swap(values):
    return lax.ppermute(values, "tp", [(0, 1), (1, 0)])


def exchange(values):
    return lax.all_to_all(values, "ctx", 0, 0, tiled=True)


def mm(left, right):
    return jnp.dot(left, right, preferred_element_type=f32)


def mm_nt(left, right):
    return lax.dot_general(left, right, (((1,), (1,)), ((), ())), preferred_element_type=f32)


def mm_tn(left, right):
    return lax.dot_general(left, right, (((0,), (0,)), ((), ())), preferred_element_type=f32)


def rms_norm(values):
    return values * lax.rsqrt(jnp.mean(values * values, -1, keepdims=True) + norm_eps)


def rotate(values, cosine, sine):
    half_size = values.shape[-1] // 2
    turned = jnp.concatenate([-values[..., half_size:], values[..., :half_size]], -1)
    return values * cosine + turned * sine


def norm_back(values, gain, upstream):
    inverse = lax.rsqrt(jnp.mean(values * values, -1, keepdims=True) + norm_eps)
    normed = values * inverse
    scaled = upstream * gain
    value_grad = inverse * (scaled - normed * jnp.mean(scaled * normed, -1, keepdims=True))
    return value_grad, jnp.sum(upstream * normed, 0)


def rope_tables(seg_row):
    length = seg_row.shape[0]
    starts = jnp.zeros((length,), jnp.int32)
    for doc in range(1, 4):
        before = jnp.sum((seg_row < doc).astype(jnp.int32))
        starts = jnp.where(seg_row == doc, before, starts)
    pos = jnp.arange(length, dtype=jnp.int32) - starts
    half_size = HD // 2
    freq_table = jnp.exp(
        jnp.arange(half_size, dtype=f32) * (-2.0 * math.log(rope_base) / HD)
    )
    angles = pos.astype(f32)[:, None] * freq_table
    cosine, sine = jnp.cos(angles), jnp.sin(angles)
    return jnp.concatenate([cosine, cosine], -1), jnp.concatenate([sine, sine], -1)


def fold(rows):
    count = rows.shape[0]
    parts = rows.reshape(count, 4, 16, 256)
    return jnp.concatenate([parts[:, i] for i in range(4)], -1)


def unfold(rows):
    count = rows.shape[0]
    return jnp.stack([rows[:, :, 256 * i : 256 * i + 256] for i in range(4)], 1).reshape(
        count, 64, 256
    )


def attend_forward(queries, keys, values, allowed):
    scores = jnp.where(allowed, mm_nt(queries, keys) * SCALE, masked_score)
    row_max = jnp.max(scores, -1, keepdims=True)
    weights_exp = jnp.exp(scores - row_max)
    row_total = jnp.sum(weights_exp, -1, keepdims=True)
    probs = weights_exp / row_total
    return mm(probs.astype(bf16), values).astype(bf16), row_max, row_total


def attend_backward(queries, keys, values, allowed, upstream, row_max, row_total):
    scores = jnp.where(allowed, mm_nt(queries, keys) * SCALE, masked_score)
    probs = jnp.exp(scores - row_max) / row_total
    value_grad = mm_tn(probs.astype(bf16), upstream)
    prob_grad = mm_nt(upstream, values)
    score_grad = (probs * (prob_grad - jnp.sum(probs * prob_grad, -1, keepdims=True))).astype(bf16)
    query_grad = mm(score_grad, keys) * SCALE
    key_grad = mm_tn(score_grad, queries) * SCALE
    return query_grad, key_grad, value_grad


def shards(
    tokens,
    cotangent,
    segments,
    w_query,
    w_key,
    w_value,
    w_output,
    w_gate,
    w_up,
    w_down,
    norm_attn,
    norm_mlp,
    norm_query,
    norm_key,
):
    core = lax.axis_index("rep") % 2
    odd = core == 1
    ctx = lax.axis_index("ctx")
    seq_role = ctx // 4

    def pick(values, axis, index):
        return lax.dynamic_index_in_dim(values, index, axis, keepdims=False)

    def by_core(own, other):
        return jnp.where(odd, other, own), jnp.where(odd, own, other)

    gate_part = pick(w_gate[0].reshape(64, 2, 768), 1, core)
    up_part = pick(w_up[0].reshape(64, 2, 768), 1, core)
    down_part = pick(w_down[0].reshape(2, 768, 64), 0, core).T
    out_part = pick(w_output[0].reshape(4, 2, HD, 64), 1, core).reshape(512, 64).T
    weights = lax.all_gather(
        jnp.concatenate([gate_part, up_part, down_part, out_part], 1), "ctx", axis=0, tiled=True
    )
    gateup_w = weights[:, :1536]
    down_wt = weights[:, 1536:2304]
    out_wt = weights[:, 2304:]

    halves = tokens.reshape(2, 2, 32, D)
    kept = pick(halves, 1, core)
    got = core_swap(pick(halves, 1, 1 - core))
    seg_other = core_swap(segments)
    cot_own = cotangent.reshape(128, D)
    cot_both = jnp.concatenate([cot_own, core_swap(cot_own)], 0)
    quad = jnp.concatenate(by_core(kept, got), 0)
    quad_send = jnp.broadcast_to(quad[:, None], (4, 4, 32, D)).reshape(16, 32, D)
    head_w = jnp.concatenate(
        [
            pick(w_query[0].reshape(64, 4, 2, HD), 2, core),
            jnp.where(odd, w_value[0], w_key[0]).reshape(64, 4, HD),
        ],
        -1,
    )
    head_w = fold(jnp.swapaxes(head_w, 0, 1))
    head_send = jnp.broadcast_to(head_w[None], (4, 4, 16, D)).reshape(16, 16, D)
    gain_row = jnp.concatenate([norm_attn[0], norm_mlp[0], norm_query[0], norm_key[0]])
    gain_send = jnp.broadcast_to(jnp.pad(gain_row, (0, D - 144)), (16, 8, D))
    fetched = exchange(jnp.concatenate([quad_send, head_send, gain_send], 1))
    token_half = fetched[:, :32]
    seq_halves = by_core(token_half, core_swap(token_half))
    seq_tokens = jnp.stack(seq_halves, 1).reshape(1024, D).astype(f32)
    qkv_w = unfold(fetched[:, 32:48]).reshape(1024, 256)
    gains = fetched[:, 48].astype(f32)
    attn_gain = gains[:, :64].reshape(D)
    mlp_gain = gains[:, 64:128].reshape(D)
    qnorm_gain = gains[:, 128:136].reshape(HD)
    knorm_gain = gains[:, 136:144].reshape(HD)

    seg_pair = jnp.where(seq_role // 2 == core, segments, seg_other)
    seg_row = pick(seg_pair, 0, seq_role % 2)
    cosine, sine = rope_tables(seg_row)
    index = jnp.arange(1024, dtype=jnp.int32)
    allowed = (seg_row[:, None] == seg_row[None, :]) & (index[None, :] <= index[:, None])

    attn_in = (rms_norm(seq_tokens) * attn_gain).astype(bf16)
    raw = mm(attn_in, qkv_w)
    query_raw, kv_raw = raw[:, :HD], raw[:, HD:]
    queries = rotate(rms_norm(query_raw) * qnorm_gain, cosine, sine).astype(bf16)
    kv_own = jnp.where(odd, kv_raw, rotate(rms_norm(kv_raw) * knorm_gain, cosine, sine)).astype(bf16)
    keys, values = by_core(kv_own, core_swap(kv_own))
    mixed_head, row_max, row_total = attend_forward(queries, keys, values, allowed)
    mixed = exchange(mixed_head.reshape(16, 64, HD)).reshape(4, 4, 64, HD)
    mixed = jnp.concatenate([mixed[:, i] for i in range(4)], -1).reshape(256, 512)

    def pair_sum(own, other):
        part = (own + core_swap(other.astype(bf16)).astype(f32)).astype(bf16)
        return part.astype(f32) + tp_swap(part).astype(f32)

    mixed_out = mm_nt(mixed, out_wt).reshape(2, 128, D)
    hidden = tokens.reshape(128, D).astype(f32)
    hidden_mid = hidden + pair_sum(pick(mixed_out, 0, core), pick(mixed_out, 0, 1 - core))

    mlp_own = (rms_norm(hidden_mid) * mlp_gain).astype(bf16)
    mlp_in = jnp.concatenate([mlp_own, core_swap(mlp_own)], 0)
    gate_up = mm(mlp_in, gateup_w)
    gate_pre, up_pre = gate_up[:, :768], gate_up[:, 768:]
    sig = jax.nn.sigmoid(gate_pre)
    act = (gate_pre * sig * up_pre).astype(bf16)
    act_grad = mm(cot_both, down_wt)
    gate_grad = (act_grad * up_pre * sig * (1.0 + gate_pre * (1.0 - sig))).astype(bf16)
    up_grad = (act_grad * (gate_pre * sig)).astype(bf16)
    gateup_grad = jnp.concatenate([gate_grad, up_grad], 1)
    mlp_back = mm_nt(gateup_grad, gateup_w)
    mlp_in_grad = pair_sum(mlp_back[:128], mlp_back[128:])
    mlp_out = mm_nt(act, down_wt)
    out_tokens = hidden_mid + pair_sum(mlp_out[:128], mlp_out[128:])
    gateup_w_grad = mm_tn(mlp_in, gateup_grad).astype(bf16)
    down_w_grad = mm_tn(cot_both, act).astype(bf16)
    mid_back, mlp_gain_grad = norm_back(hidden_mid, mlp_gain, mlp_in_grad)
    grad = cot_own.astype(f32) + mid_back
    grad_own = grad.astype(bf16)
    grad_low = jnp.concatenate(by_core(grad_own, core_swap(grad_own)), 0)
    mixed_grad = mm(grad_low, out_wt).astype(bf16).reshape(4, 64, 4, HD)
    mixed_grad = exchange(jnp.swapaxes(mixed_grad, 1, 2).reshape(16, 64, HD)).reshape(1024, HD)
    out_w_grad = mm_tn(grad_low, mixed).astype(bf16)

    query_grad, key_part, value_part = attend_backward(
        queries, keys, values, allowed, mixed_grad, row_max, row_total
    )
    kv_grad = jnp.where(odd, value_part, key_part) + core_swap(
        jnp.where(odd, key_part, value_part)
    )
    query_back, qgain_grad = norm_back(query_raw, qnorm_gain, rotate(query_grad, cosine, -sine))
    key_back, kgain_grad = norm_back(kv_raw, knorm_gain, rotate(kv_grad, cosine, -sine))
    kgain_grad = jnp.where(odd, 0.0, kgain_grad)
    raw_grad = jnp.concatenate(
        [query_back.astype(bf16), jnp.where(odd, kv_grad, key_back).astype(bf16)], 1
    )
    in_part = mm_nt(raw_grad, qkv_w)
    attn_gain_grad = jnp.sum(in_part * rms_norm(seq_tokens), 0)
    in_part = in_part.reshape(16, 2, 32, D)
    in_pair = pick(in_part, 1, core) + core_swap(pick(in_part, 1, 1 - core).astype(bf16)).astype(
        f32
    )
    qkv_w_grad = mm_tn(attn_in, raw_grad).astype(bf16)
    gain_grads = jnp.concatenate(
        [
            attn_gain_grad.reshape(16, 64),
            (0.5 * mlp_gain_grad).reshape(16, 64),
            qgain_grad.reshape(16, 8),
            kgain_grad.reshape(16, 8),
        ],
        1,
    ).astype(bf16)
    gain_grads = jnp.pad(gain_grads[:, None], ((0, 0), (0, 7), (0, D - 144)))
    returned = exchange(
        jnp.concatenate(
            [in_pair.astype(bf16), fold(qkv_w_grad.reshape(16, 64, 256)), gain_grads], 1
        )
    )
    in_sum = jnp.sum(returned[:, :32].reshape(4, 4, 32, D).astype(f32), 1).astype(bf16)
    in_sum = in_sum.astype(f32) + tp_swap(in_sum).astype(f32)
    in_sum = in_sum.reshape(2, 2, 32, D)
    in_own = by_core(pick(in_sum, 0, core), core_swap(pick(in_sum, 0, 1 - core)))
    attn_in_grad = jnp.stack(in_own, 1).reshape(128, D)
    input_back, _ = norm_back(hidden, attn_gain, attn_in_grad)
    tokens_grad = grad + input_back

    def owned(part):
        total = jnp.sum(exchange(part.reshape(16, 64, -1)).astype(f32), 0).astype(bf16)
        return total.astype(f32) + zlo_swap(total).astype(f32)

    def both(part):
        return by_core(part, core_swap(part))

    down_grads = both(owned(down_w_grad))
    gateup_grads = both(owned(gateup_w_grad))
    out_grads = both(owned(out_w_grad))
    qkv_sum = jnp.sum(unfold(returned[:, 32:48]).reshape(4, 4, 64, 256).astype(f32), 0).astype(bf16)
    qkv_sum = qkv_sum.astype(f32) + zlo_swap(qkv_sum).astype(f32)
    qkv_grads = both(qkv_sum)
    gain_sum = jnp.sum(returned[:, 48, :256].astype(f32), 0)
    gain_sum = gain_sum + tp_swap(gain_sum)
    gain_sum = gain_sum + zlo_swap(gain_sum)
    gain_sum = gain_sum + core_swap(gain_sum)

    def wide(part):
        return jnp.swapaxes(part, 0, 1).reshape(64, 512)

    query_w_grad = jnp.stack([part[:, :, :HD] for part in qkv_grads], 2)
    query_w_grad = jnp.swapaxes(query_w_grad, 0, 1).reshape(1, 64, 1024)
    out_w_grad = jnp.stack([part.T.reshape(4, HD, 64) for part in out_grads], 1).reshape(1024, 64)
    return (
        out_tokens.reshape(2, 64, D),
        tokens_grad.reshape(2, 64, D),
        query_w_grad,
        wide(qkv_grads[0][:, :, HD:])[None],
        wide(qkv_grads[1][:, :, HD:])[None],
        out_w_grad[None],
        jnp.concatenate([part[:, :768] for part in gateup_grads], 1)[None],
        jnp.concatenate([part[:, 768:] for part in gateup_grads], 1)[None],
        jnp.concatenate([part.T for part in down_grads], 0)[None],
        gain_sum[None, :64],
        gain_sum[None, 64:128],
        gain_sum[None, 128:136],
        gain_sum[None, 136:144],
    )


def solution(mesh):
    rows = P(None, "ctx", "tp")
    columns = P(None, "tp", "ctx")
    gain = P(None, "ctx")
    token = P("rep", "ctx", None)
    weight_specs = (rows, rows, rows, columns, rows, rows, columns, gain, gain, gain, gain)
    return jax.shard_map(
        shards,
        mesh=mesh,
        in_specs=(token, token, P("rep", None)) + weight_specs,
        out_specs=(token, token) + weight_specs,
        check_vma=False,
    )
```

```python
import math

import jax
import jax.numpy as jnp
from jax import lax
from jax.experimental import pallas as pl
from jax.experimental.pallas import tpu as pltpu
from jax.sharding import PartitionSpec as P

HD = 128
D = 1024
SCALE = 1.0 / math.sqrt(HD)
norm_eps = 1e-06
rope_base = 1000000.0
masked_score = -1e30
bf16 = jnp.bfloat16
f32 = jnp.float32


def core_swap(values):
    return lax.ppermute(values, "rep", [(0, 1), (1, 0), (2, 3), (3, 2)])


def zlo_swap(values):
    return lax.ppermute(values, "rep", [(0, 2), (1, 3), (2, 0), (3, 1)])


def tp_swap(values):
    return lax.ppermute(values, "tp", [(0, 1), (1, 0)])


def exchange(values):
    return lax.all_to_all(values, "ctx", 0, 0, tiled=True)


def mm(left, right):
    return jnp.dot(left, right, preferred_element_type=f32)


def mm_nt(left, right):
    return lax.dot_general(left, right, (((1,), (1,)), ((), ())), preferred_element_type=f32)


def mm_tn(left, right):
    return lax.dot_general(left, right, (((0,), (0,)), ((), ())), preferred_element_type=f32)


def rms_norm(values):
    return values * lax.rsqrt(jnp.mean(values * values, -1, keepdims=True) + norm_eps)


def norm_back(values, gain, upstream):
    inverse = lax.rsqrt(jnp.mean(values * values, -1, keepdims=True) + norm_eps)
    normed = values * inverse
    scaled = upstream * gain
    value_grad = inverse * (scaled - normed * jnp.mean(scaled * normed, -1, keepdims=True))
    return value_grad, jnp.sum(upstream * normed, 0, keepdims=True)


def rotate(values, cosine, sine):
    return values * cosine + pltpu.roll(values, HD // 2, 1) * sine


def rotate_back(values, cosine, sine):
    return values * cosine - pltpu.roll(values, HD // 2, 1) * sine


def kernel_call(body, out_shape, flops, *operands):
    return kernel_call_scratch(body, out_shape, [], flops, *operands)


def kernel_call_scratch(body, out_shape, scratch, flops, *operands):
    specs = [pl.BlockSpec(memory_space=pltpu.SMEM)]
    specs += [pl.BlockSpec(memory_space=pltpu.VMEM)] * (len(operands) - 1)
    size = sum(math.prod(x.shape) * x.dtype.itemsize for x in list(operands) + list(out_shape))
    return pl.pallas_call(
        body,
        out_shape=out_shape,
        in_specs=specs,
        out_specs=[pl.BlockSpec(memory_space=pltpu.VMEM)] * len(out_shape),
        scratch_shapes=scratch,
        cost_estimate=pl.CostEstimate(flops=flops, bytes_accessed=size, transcendentals=0),
        compiler_params=pltpu.CompilerParams(vmem_limit_bytes=48 << 20),
    )(*operands)


def shape(dims, dtype):
    return jax.ShapeDtypeStruct(dims, dtype)


BLOCK = 256


def masked_scores(queries, keys, seg_column, seg_row, start, length):
    row = start + lax.broadcasted_iota(jnp.int32, (BLOCK, length), 0)
    column = lax.broadcasted_iota(jnp.int32, (BLOCK, length), 1)
    allowed = (seg_column == seg_row) & (column <= row)
    return jnp.where(allowed, mm_nt(queries, keys) * SCALE, masked_score)


def attend_kernel(odd, q_ref, own_ref, other_ref, segc_ref, segr_ref, mixed_ref, lse_ref):
    own, other = own_ref[...], other_ref[...]
    flag = odd[0] == 1
    keys, values = jnp.where(flag, other, own), jnp.where(flag, own, other)
    for start in range(0, 1024, BLOCK):
        rows = slice(start, start + BLOCK)
        length = start + BLOCK
        scores = masked_scores(
            q_ref[rows], keys[:length], segc_ref[rows], segr_ref[:, :length], start, length
        )
        row_max = jnp.max(scores, -1, keepdims=True)
        weights_exp = jnp.exp(scores - row_max)
        row_total = jnp.sum(weights_exp, -1, keepdims=True)
        probs = (weights_exp * (1.0 / row_total)).astype(bf16)
        mixed_ref[rows] = mm(probs, values[:length]).astype(bf16)
        lse_ref[rows] = row_max + jnp.log(row_total)


def attend_back_kernel(
    odd,
    q_ref,
    own_ref,
    other_ref,
    segc_ref,
    segr_ref,
    lse_ref,
    up_ref,
    raw_ref,
    gain_ref,
    cos_ref,
    sin_ref,
    keep_ref,
    give_ref,
    low_ref,
    gain_grad_ref,
    key_sum,
    value_sum,
):
    own, other = own_ref[...], other_ref[...]
    flag = odd[0] == 1
    keys, values = jnp.where(flag, other, own), jnp.where(flag, own, other)
    gain_grad = jnp.zeros((1, HD), f32)
    for start in range(1024 - BLOCK, -1, -BLOCK):
        rows = slice(start, start + BLOCK)
        length = start + BLOCK
        queries, upstream = q_ref[rows], up_ref[rows]
        scores = masked_scores(
            queries, keys[:length], segc_ref[rows], segr_ref[:, :length], start, length
        )
        probs = jnp.exp(scores - lse_ref[rows])
        value_part = mm_tn(probs.astype(bf16), upstream)
        prob_grad = mm_nt(upstream, values[:length])
        score_grad = (
            probs * (prob_grad - jnp.sum(probs * prob_grad, -1, keepdims=True))
        ).astype(bf16)
        key_part = mm_tn(score_grad, queries)
        if length == 1024:
            value_sum[...] = value_part
            key_sum[...] = key_part
        else:
            value_sum[:length] += value_part
            key_sum[:length] += key_part
        query_grad = mm(score_grad, keys[:length]) * SCALE
        back, part = norm_back(
            raw_ref[rows], gain_ref[...], rotate_back(query_grad, cos_ref[rows], sin_ref[rows])
        )
        low_ref[rows] = back.astype(bf16)
        gain_grad += part
    gain_grad_ref[...] = gain_grad
    key_grad, value_grad = key_sum[...] * SCALE, value_sum[...]
    keep_ref[...] = jnp.where(flag, value_grad, key_grad)
    give_ref[...] = jnp.where(flag, key_grad, value_grad)


def project_back_kernel(
    odd,
    keep_ref,
    got_ref,
    raw_ref,
    gain_ref,
    cos_ref,
    sin_ref,
    low_ref,
    in_ref,
    tokens_ref,
    w_ref,
    half_ref,
    give_ref,
    fold_ref,
    attn_gain_ref,
    gain_grad_ref,
):
    flag = odd[0] == 1
    total = keep_ref[...] + got_ref[...]
    back, part = norm_back(
        raw_ref[...], gain_ref[...], rotate_back(total, cos_ref[...], sin_ref[...])
    )
    gain_grad_ref[...] = jnp.where(flag, 0.0, part)
    raw_grad = jnp.concatenate([low_ref[...], jnp.where(flag, total, back).astype(bf16)], 1)
    attn_gain = jnp.zeros((1, D), f32)
    for start in range(0, 1024, BLOCK):
        rows = slice(start, start + BLOCK)
        blocks = slice(start // 64, (start + BLOCK) // 64)
        in_part = mm_nt(raw_grad[rows], w_ref[...])
        attn_gain += jnp.sum(in_part * rms_norm(tokens_ref[rows].astype(f32)), 0, keepdims=True)
        halves = in_part.reshape(4, 2, 32, D)
        half_ref[blocks] = jnp.where(flag, halves[:, 1], halves[:, 0])
        give_ref[blocks] = jnp.where(flag, halves[:, 0], halves[:, 1]).astype(bf16)
        w_grad = mm_tn(in_ref[:, rows], raw_grad).astype(bf16).reshape(4, 4, 16, 256)
        for i in range(4):
            fold_ref[blocks, :, 256 * i : 256 * i + 256] = w_grad[:, i]
    attn_gain_ref[...] = attn_gain


def mlp_grad_kernel(zero, in_ref, up_ref, cot_ref, act_ref, out_ref):
    for start in range(0, D, BLOCK):
        rows = slice(start, start + BLOCK)
        out_ref[rows, :1536] = mm_tn(in_ref[:, rows], up_ref[...]).astype(bf16)
        out_ref[rows, 1536:] = mm_tn(cot_ref[:, rows], act_ref[...]).astype(bf16)


def rope_tables(seg_row):
    length = seg_row.shape[0]
    starts = jnp.zeros((length,), jnp.int32)
    for doc in range(1, 4):
        before = jnp.sum((seg_row < doc).astype(jnp.int32))
        starts = jnp.where(seg_row == doc, before, starts)
    pos = jnp.arange(length, dtype=jnp.int32) - starts
    half_size = HD // 2
    freq_table = jnp.exp(
        jnp.arange(half_size, dtype=f32) * (-2.0 * math.log(rope_base) / HD)
    )
    angles = pos.astype(f32)[:, None] * freq_table
    cosine, sine = jnp.cos(angles), jnp.sin(angles)
    return jnp.concatenate([cosine, cosine], -1), jnp.concatenate([-sine, sine], -1)


def after(values, *others):
    return lax.optimization_barrier((values,) + others)[0]


def fold(rows):
    count = rows.shape[0]
    parts = rows.reshape(count, 4, 16, 256)
    return jnp.concatenate([parts[:, i] for i in range(4)], -1)


def unfold(rows):
    count = rows.shape[0]
    return jnp.stack([rows[:, :, 256 * i : 256 * i + 256] for i in range(4)], 1).reshape(
        count, 64, 256
    )


def shards(
    tokens,
    cotangent,
    segments,
    w_query,
    w_key,
    w_value,
    w_output,
    w_gate,
    w_up,
    w_down,
    norm_attn,
    norm_mlp,
    norm_query,
    norm_key,
):
    core = lax.axis_index("rep") % 2
    odd = core == 1
    ctx = lax.axis_index("ctx")
    seq_role = ctx // 4

    def pick(values, axis, index):
        return lax.dynamic_index_in_dim(values, index, axis, keepdims=False)

    def by_core(own, other):
        return jnp.where(odd, other, own), jnp.where(odd, own, other)

    def lanes(values, count, size):
        return [
            jnp.where(
                odd,
                values[:, (2 * i + 1) * size : (2 * i + 2) * size],
                values[:, 2 * i * size : (2 * i + 1) * size],
            )
            for i in range(count)
        ]

    halves = tokens.reshape(2, 2, 32, D)
    kept = pick(halves, 1, core)
    got = core_swap(pick(halves, 1, 1 - core))
    quad = jnp.concatenate(by_core(kept, got), 0)
    quad_send = jnp.broadcast_to(quad[:, None], (4, 4, 32, D)).reshape(16, 32, D)
    query_parts = lanes(w_query[0], 4, HD)
    kv_w = jnp.where(odd, w_value[0], w_key[0])
    head_w = jnp.stack(
        [
            jnp.concatenate([query_parts[i], kv_w[:, i * HD : (i + 1) * HD]], 1)
            for i in range(4)
        ]
    )
    head_send = jnp.broadcast_to(fold(head_w)[None], (4, 4, 16, D)).reshape(16, 16, D)
    gain_row = jnp.concatenate([norm_attn[0], norm_mlp[0], norm_query[0], norm_key[0]])
    gain_send = jnp.broadcast_to(jnp.pad(gain_row, (0, D - 144)), (16, 8, D))
    fetched = exchange(jnp.concatenate([quad_send, head_send, gain_send], 1))
    seg_other = core_swap(segments)
    cot_own = cotangent.reshape(128, D)
    cot_both = jnp.concatenate([cot_own, core_swap(cot_own)], 0)

    w_gate, w_up, w_down, w_output, _ = lax.optimization_barrier(
        (w_gate, w_up, w_down, w_output, got)
    )
    out_part = jnp.concatenate(
        [
            jnp.where(
                odd,
                w_output[0, (2 * i + 1) * HD : (2 * i + 2) * HD],
                w_output[0, 2 * i * HD : (2 * i + 1) * HD],
            )
            for i in range(4)
        ],
        0,
    )
    down_part = jnp.where(odd, w_down[0, 768:], w_down[0, :768])
    weights = lax.all_gather(
        jnp.concatenate(
            lanes(w_gate[0], 1, 768) + lanes(w_up[0], 1, 768) + [down_part.T, out_part.T], 1
        ),
        "ctx",
        axis=0,
        tiled=True,
    )
    gateup_w = weights[:, :1536]
    down_wt = weights[:, 1536:2304]
    out_wt = weights[:, 2304:]

    token_half = fetched[:, :32]
    seq_halves = by_core(token_half, core_swap(token_half))
    seq_tokens = jnp.stack(seq_halves, 1).reshape(1024, D)
    qkv_w = unfold(fetched[:, 32:48]).reshape(1024, 256)
    gains = fetched[:, 48].astype(f32)
    attn_gain = gains[:, :64].reshape(D)
    mlp_gain = gains[:, 64:128].reshape(D)
    qnorm_gain = gains[:, 128:136].reshape(HD)
    knorm_gain = gains[:, 136:144].reshape(HD)

    seg_pair = jnp.where(seq_role // 2 == core, segments, seg_other)
    seg_row = pick(seg_pair, 0, seq_role % 2)
    cosine, sine = rope_tables(seg_row)
    seg_column, seg_row = seg_row[:, None], seg_row[None, :]
    flag = core.reshape(1)

    def rope(values):
        turned = jnp.concatenate([values[:, HD // 2 :], values[:, : HD // 2]], -1)
        return values * cosine + turned * sine

    attn_in = (rms_norm(seq_tokens.astype(f32)) * attn_gain).astype(bf16)
    raw = mm(attn_in, qkv_w)
    query_raw, kv_raw = raw[:, :HD], raw[:, HD:]
    queries = rope(rms_norm(query_raw) * qnorm_gain).astype(bf16)
    kv_own = jnp.where(odd, kv_raw, rope(rms_norm(kv_raw) * knorm_gain)).astype(bf16)
    kv_other = core_swap(kv_own)
    mixed_head, lse = kernel_call(
        attend_kernel,
        [shape((1024, HD), bf16), shape((1024, 1), f32)],
        4 * 640 * 1024 * HD,
        flag,
        queries,
        kv_own,
        kv_other,
        seg_column,
        seg_row,
    )
    mixed = exchange(after(mixed_head, cot_both).reshape(16, 64, HD)).reshape(4, 4, 64, HD)
    mixed = jnp.concatenate([mixed[:, i] for i in range(4)], -1).reshape(256, 512)

    def pair_sum(own, other):
        part = (own + core_swap(other.astype(bf16)).astype(f32)).astype(bf16)
        return part.astype(f32) + tp_swap(part).astype(f32)

    mixed_out = mm_nt(mixed, out_wt).reshape(2, 128, D)
    hidden = tokens.reshape(128, D).astype(f32)
    hidden_mid = hidden + pair_sum(pick(mixed_out, 0, core), pick(mixed_out, 0, 1 - core))

    mlp_own = (rms_norm(hidden_mid) * mlp_gain).astype(bf16)
    mlp_in = jnp.concatenate([mlp_own, core_swap(mlp_own)], 0)
    gate_up = mm(mlp_in, gateup_w)
    gate_pre, up_pre = gate_up[:, :768], gate_up[:, 768:]
    sig = jax.nn.sigmoid(gate_pre)
    act = (gate_pre * sig * up_pre).astype(bf16)
    act_grad = mm(cot_both, down_wt)
    gate_grad = (act_grad * up_pre * sig * (1.0 + gate_pre * (1.0 - sig))).astype(bf16)
    up_grad = (act_grad * (gate_pre * sig)).astype(bf16)
    gateup_grad = jnp.concatenate([gate_grad, up_grad], 1)
    mlp_back = mm_nt(gateup_grad, gateup_w)
    mlp_in_grad = pair_sum(mlp_back[:128], mlp_back[128:])
    mlp_w_grad = kernel_call(
        mlp_grad_kernel,
        [shape((D, 2304), bf16)],
        2 * 256 * 2304 * D,
        flag,
        mlp_in,
        gateup_grad,
        cot_both,
        act,
    )[0]
    mlp_w_grad = lax.psum_scatter(mlp_w_grad, "ctx", scatter_dimension=0, tiled=True)
    mid_back, mlp_gain_grad = norm_back(hidden_mid, mlp_gain, mlp_in_grad)
    grad = cot_own.astype(f32) + mid_back
    grad_own = grad.astype(bf16)
    grad_low = jnp.concatenate(by_core(grad_own, core_swap(grad_own)), 0)
    mixed_grad = mm(grad_low, out_wt).astype(bf16)
    mixed_grad = jnp.concatenate(
        [
            mixed_grad[64 * i : 64 * i + 64, HD * j : HD * j + HD]
            for i in range(4)
            for j in range(4)
        ],
        0,
    )
    mixed_grad = exchange(mixed_grad.reshape(16, 64, HD)).reshape(1024, HD)
    mlp_out = mm_nt(after(act, mixed_grad), down_wt)
    out_tokens = hidden_mid + pair_sum(mlp_out[:128], mlp_out[128:])
    out_w_grad = mm_tn(after(grad_low, mixed_grad), mixed).astype(bf16)
    out_w_grad = jnp.sum(exchange(out_w_grad.reshape(16, 64, 512)).astype(f32), 0).astype(bf16)

    kv_keep, kv_give, query_low, qgain_grad = kernel_call_scratch(
        attend_back_kernel,
        [
            shape((1024, HD), f32),
            shape((1024, HD), f32),
            shape((1024, HD), bf16),
            shape((1, HD), f32),
        ],
        [pltpu.VMEM((1024, HD), f32), pltpu.VMEM((1024, HD), f32)],
        10 * 640 * 1024 * HD,
        flag,
        queries,
        kv_own,
        kv_other,
        seg_column,
        seg_row,
        lse,
        mixed_grad,
        query_raw,
        qnorm_gain[None],
        cosine,
        sine,
    )
    in_half, in_give, qkv_fold, attn_gain_grad, kgain_grad = kernel_call(
        project_back_kernel,
        [
            shape((16, 32, D), f32),
            shape((16, 32, D), bf16),
            shape((16, 16, D), bf16),
            shape((1, D), f32),
            shape((1, HD), f32),
        ],
        4 * 1024 * 1024 * 256,
        flag,
        kv_keep,
        core_swap(kv_give),
        kv_raw,
        knorm_gain[None],
        cosine,
        sine,
        query_low,
        attn_in,
        seq_tokens,
        qkv_w,
    )
    in_pair = in_half + core_swap(in_give).astype(f32)
    gain_grads = jnp.concatenate(
        [
            attn_gain_grad.reshape(16, 64),
            (0.5 * mlp_gain_grad).reshape(16, 64),
            qgain_grad.reshape(16, 8),
            kgain_grad.reshape(16, 8),
        ],
        1,
    ).astype(bf16)
    gain_grads = jnp.pad(gain_grads[:, None], ((0, 0), (0, 7), (0, D - 144)))
    returned = exchange(
        after(
            jnp.concatenate([in_pair.astype(bf16), qkv_fold, gain_grads], 1),
            out_tokens,
            out_w_grad,
        )
    )
    in_sum = jnp.sum(returned[:, :32].reshape(4, 4, 32, D).astype(f32), 1).reshape(128, D)
    gain_sum = jnp.sum(returned[:, 48:].astype(f32), 0)
    in_sum = jnp.concatenate([in_sum, gain_sum, jnp.zeros((8, D), f32)], 0).astype(bf16)
    in_sum = in_sum.astype(f32) + tp_swap(in_sum).astype(f32)
    gain_sum = in_sum[128, :256]
    in_sum = in_sum[:128].reshape(2, 2, 32, D)
    in_own = by_core(pick(in_sum, 0, core), core_swap(pick(in_sum, 0, 1 - core)))
    attn_in_grad = jnp.stack(in_own, 1).reshape(128, D)
    input_back, _ = norm_back(hidden, attn_gain, attn_in_grad)
    tokens_grad = grad + input_back

    def owned(part):
        return part.astype(f32) + zlo_swap(part).astype(f32)

    def both(part):
        return by_core(part, core_swap(part))

    mlp_grads = both(owned(mlp_w_grad))
    out_grads = both(owned(out_w_grad))
    qkv_sum = jnp.sum(unfold(returned[:, 32:48]).reshape(4, 4, 64, 256).astype(f32), 0)
    qkv_grads = both(owned(qkv_sum.astype(bf16)))
    gain_sum = gain_sum + zlo_swap(gain_sum)
    gain_sum = gain_sum + core_swap(gain_sum)

    even_qkv, odd_qkv = qkv_grads
    query_w_grad = [part[i, :, :HD] for i in range(4) for part in qkv_grads]
    out_w_grad = [part.T[i * HD : (i + 1) * HD] for i in range(4) for part in out_grads]
    return (
        out_tokens.reshape(2, 64, D),
        tokens_grad.reshape(2, 64, D),
        jnp.concatenate(query_w_grad, 1)[None],
        jnp.concatenate([even_qkv[i, :, HD:] for i in range(4)], 1)[None],
        jnp.concatenate([odd_qkv[i, :, HD:] for i in range(4)], 1)[None],
        jnp.concatenate(out_w_grad, 0)[None],
        jnp.concatenate([part[:, :768] for part in mlp_grads], 1)[None],
        jnp.concatenate([part[:, 768:1536] for part in mlp_grads], 1)[None],
        jnp.concatenate([part[:, 1536:].T for part in mlp_grads], 0)[None],
        gain_sum[None, :64],
        gain_sum[None, 64:128],
        gain_sum[None, 128:136],
        gain_sum[None, 136:144],
    )


def solution(mesh):
    rows = P(None, "ctx", "tp")
    columns = P(None, "tp", "ctx")
    gain = P(None, "ctx")
    token = P("rep", "ctx", None)
    weight_specs = (rows, rows, rows, columns, rows, rows, columns, gain, gain, gain, gain)
    return jax.shard_map(
        shards,
        mesh=mesh,
        in_specs=(token, token, P("rep", None)) + weight_specs,
        out_specs=(token, token) + weight_specs,
        check_vma=False,
    )
```

```python
import math

import jax
import jax.numpy as jnp
from jax import lax
from jax.experimental import pallas as pl
from jax.experimental.pallas import tpu as pltpu
from jax.sharding import PartitionSpec as P

HD = 128
D = 1024
SCALE = 1.0 / math.sqrt(HD)
norm_eps = 1e-06
rope_base = 1000000.0
masked_score = -1e30
bf16 = jnp.bfloat16
f32 = jnp.float32


def core_swap(values):
    return lax.ppermute(values, "rep", [(0, 1), (1, 0), (2, 3), (3, 2)])


def zlo_swap(values):
    return lax.ppermute(values, "rep", [(0, 2), (1, 3), (2, 0), (3, 1)])


def tp_swap(values):
    return lax.ppermute(values, "tp", [(0, 1), (1, 0)])


def exchange(values):
    return lax.all_to_all(values, "ctx", 0, 0, tiled=True)


def mm(left, right):
    return jnp.dot(left, right, preferred_element_type=f32)


def mm_nt(left, right):
    return lax.dot_general(left, right, (((1,), (1,)), ((), ())), preferred_element_type=f32)


def mm_tn(left, right):
    return lax.dot_general(left, right, (((0,), (0,)), ((), ())), preferred_element_type=f32)


def rms_norm(values):
    return values * lax.rsqrt(jnp.mean(values * values, -1, keepdims=True) + norm_eps)


def norm_back(values, gain, upstream):
    inverse = lax.rsqrt(jnp.mean(values * values, -1, keepdims=True) + norm_eps)
    normed = values * inverse
    scaled = upstream * gain
    value_grad = inverse * (scaled - normed * jnp.mean(scaled * normed, -1, keepdims=True))
    return value_grad, jnp.sum(upstream * normed, 0, keepdims=True)


def rotate(values, cosine, sine):
    return values * cosine + pltpu.roll(values, HD // 2, 1) * sine


def rotate_back(values, cosine, sine):
    return values * cosine - pltpu.roll(values, HD // 2, 1) * sine


def kernel_call(body, out_shape, flops, *operands):
    return kernel_call_scratch(body, out_shape, [], flops, *operands)


def kernel_call_scratch(body, out_shape, scratch, flops, *operands):
    specs = [pl.BlockSpec(memory_space=pltpu.SMEM)]
    specs += [pl.BlockSpec(memory_space=pltpu.VMEM)] * (len(operands) - 1)
    size = sum(math.prod(x.shape) * x.dtype.itemsize for x in list(operands) + list(out_shape))
    return pl.pallas_call(
        body,
        out_shape=out_shape,
        in_specs=specs,
        out_specs=[pl.BlockSpec(memory_space=pltpu.VMEM)] * len(out_shape),
        scratch_shapes=scratch,
        cost_estimate=pl.CostEstimate(flops=flops, bytes_accessed=size, transcendentals=0),
        compiler_params=pltpu.CompilerParams(vmem_limit_bytes=48 << 20),
    )(*operands)


def shape(dims, dtype):
    return jax.ShapeDtypeStruct(dims, dtype)


BLOCK = 256


def masked_scores(queries, keys, seg_column, seg_row, start, length):
    row = start + lax.broadcasted_iota(jnp.int32, (BLOCK, length), 0)
    column = lax.broadcasted_iota(jnp.int32, (BLOCK, length), 1)
    allowed = (seg_column == seg_row) & (column <= row)
    return jnp.where(allowed, mm_nt(queries, keys) * SCALE, masked_score)


def attend_kernel(odd, q_ref, own_ref, other_ref, segc_ref, segr_ref, mixed_ref, lse_ref):
    own, other = own_ref[...], other_ref[...]
    flag = odd[0] == 1
    keys, values = jnp.where(flag, other, own), jnp.where(flag, own, other)
    for start in range(0, 1024, BLOCK):
        rows = slice(start, start + BLOCK)
        length = start + BLOCK
        scores = masked_scores(
            q_ref[rows], keys[:length], segc_ref[rows], segr_ref[:, :length], start, length
        )
        row_max = jnp.max(scores, -1, keepdims=True)
        weights_exp = jnp.exp(scores - row_max)
        row_total = jnp.sum(weights_exp, -1, keepdims=True)
        probs = (weights_exp * (1.0 / row_total)).astype(bf16)
        mixed_ref[rows] = mm(probs, values[:length]).astype(bf16)
        lse_ref[rows] = row_max + jnp.log(row_total)


def attend_back_kernel(
    odd,
    q_ref,
    own_ref,
    other_ref,
    segc_ref,
    segr_ref,
    lse_ref,
    up_ref,
    raw_ref,
    gain_ref,
    rope_ref,
    keep_ref,
    give_ref,
    low_ref,
    gain_grad_ref,
    key_sum,
    value_sum,
):
    own, other = own_ref[...], other_ref[...]
    flag = odd[0] == 1
    keys, values = jnp.where(flag, other, own), jnp.where(flag, own, other)
    gain_grad = jnp.zeros((1, HD), f32)
    for start in range(1024 - BLOCK, -1, -BLOCK):
        rows = slice(start, start + BLOCK)
        length = start + BLOCK
        queries, upstream = q_ref[rows], up_ref[rows]
        scores = masked_scores(
            queries, keys[:length], segc_ref[rows], segr_ref[:, :length], start, length
        )
        probs = jnp.exp(scores - lse_ref[rows])
        value_part = mm_tn(probs.astype(bf16), upstream)
        prob_grad = mm_nt(upstream, values[:length])
        score_grad = (
            probs * (prob_grad - jnp.sum(probs * prob_grad, -1, keepdims=True))
        ).astype(bf16)
        key_part = mm_tn(score_grad, queries)
        if length == 1024:
            value_sum[...] = value_part
            key_sum[...] = key_part
        else:
            value_sum[:length] += value_part
            key_sum[:length] += key_part
        query_grad = mm(score_grad, keys[:length]) * SCALE
        back, part = norm_back(
            raw_ref[rows, :HD],
            gain_ref[...],
            rotate_back(query_grad, rope_ref[rows, :HD], rope_ref[rows, HD:]),
        )
        low_ref[rows] = back.astype(bf16)
        gain_grad += part
    gain_grad_ref[...] = gain_grad
    key_grad, value_grad = key_sum[...] * SCALE, value_sum[...]
    keep_ref[...] = jnp.where(flag, value_grad, key_grad)
    give_ref[...] = jnp.where(flag, key_grad, value_grad)


def project_back_kernel(
    odd,
    keep_ref,
    got_ref,
    raw_ref,
    gain_ref,
    rope_ref,
    low_ref,
    tokens_ref,
    more_tokens_ref,
    token_gain_ref,
    w_ref,
    half_ref,
    give_ref,
    fold_ref,
    attn_gain_ref,
    gain_grad_ref,
    attn_in,
):
    flag = odd[0] == 1
    total = keep_ref[...] + got_ref[...]
    back, part = norm_back(
        raw_ref[:, HD:],
        gain_ref[...],
        rotate_back(total, rope_ref[:, :HD], rope_ref[:, HD:]),
    )
    gain_grad_ref[...] = jnp.where(flag, 0.0, part)
    raw_grad = jnp.concatenate([low_ref[...], jnp.where(flag, total, back).astype(bf16)], 1)
    attn_gain = jnp.zeros((1, D), f32)
    for start in range(0, 1024, BLOCK):
        rows = slice(start, start + BLOCK)
        blocks = slice(start // 64, (start + BLOCK) // 64)
        in_part = mm_nt(raw_grad[rows], w_ref[...])
        held, more = tokens_ref[blocks], more_tokens_ref[blocks]
        tokens = jnp.stack([jnp.where(flag, more, held), jnp.where(flag, held, more)], 1)
        normed = rms_norm(tokens.reshape(BLOCK, D).astype(f32))
        attn_in[rows] = (normed * token_gain_ref[...]).astype(bf16)
        attn_gain += jnp.sum(in_part * normed, 0, keepdims=True)
        halves = in_part.reshape(4, 2, 32, D)
        half_ref[blocks] = jnp.where(flag, halves[:, 1], halves[:, 0])
        give_ref[blocks] = jnp.where(flag, halves[:, 0], halves[:, 1]).astype(bf16)
    for start in range(0, D, BLOCK):
        rows = slice(start, start + BLOCK)
        blocks = slice(start // 64, (start + BLOCK) // 64)
        w_grad = mm_tn(attn_in[:, rows], raw_grad).astype(bf16).reshape(4, 4, 16, 256)
        for i in range(4):
            fold_ref[blocks, :, 256 * i : 256 * i + 256] = w_grad[:, i]
    attn_gain_ref[...] = attn_gain


def mlp_grad_kernel(unused, in_ref, up_ref, cot_ref, act_ref, out_ref):
    for start in range(0, D, BLOCK):
        rows = slice(start, start + BLOCK)
        out_ref[rows, :1536] = mm_tn(in_ref[:, rows], up_ref[...]).astype(bf16)
        out_ref[rows, 1536:] = mm_tn(cot_ref[:, rows], act_ref[...]).astype(bf16)


def mixed_grad_kernel(unused, grad_ref, w_ref, out_ref):
    out = mm(grad_ref[...], w_ref[...]).astype(bf16)
    for i in range(4):
        for j in range(4):
            out_ref[4 * i + j] = out[64 * i : 64 * i + 64, HD * j : HD * j + HD]


def rope_tables(seg_row):
    length = seg_row.shape[0]
    starts = jnp.zeros((length,), jnp.int32)
    for doc in range(1, 4):
        before = jnp.sum((seg_row < doc).astype(jnp.int32))
        starts = jnp.where(seg_row == doc, before, starts)
    pos = jnp.arange(length, dtype=jnp.int32) - starts
    half_size = HD // 2
    freq_table = jnp.exp(
        jnp.arange(half_size, dtype=f32) * (-2.0 * math.log(rope_base) / HD)
    )
    angles = pos.astype(f32)[:, None] * freq_table
    cosine, sine = jnp.cos(angles), jnp.sin(angles)
    return jnp.concatenate([cosine, cosine], -1), jnp.concatenate([-sine, sine], -1)


def after(values, *others):
    return lax.optimization_barrier((values,) + others)[0]


def fold(rows):
    count = rows.shape[0]
    parts = rows.reshape(count, 4, 16, 256)
    return jnp.concatenate([parts[:, i] for i in range(4)], -1)


def unfold(rows):
    count = rows.shape[0]
    return jnp.stack([rows[:, :, 256 * i : 256 * i + 256] for i in range(4)], 1).reshape(
        count, 64, 256
    )


def shards(
    tokens,
    cotangent,
    segments,
    w_query,
    w_key,
    w_value,
    w_output,
    w_gate,
    w_up,
    w_down,
    norm_attn,
    norm_mlp,
    norm_query,
    norm_key,
):
    rep = lax.axis_index("rep")
    core = rep % 2
    odd = core == 1
    far = rep // 2 == 1
    ctx = lax.axis_index("ctx")
    seq_role = ctx // 4

    def pick(values, axis, index):
        return lax.dynamic_index_in_dim(values, index, axis, keepdims=False)

    def by_core(own, other):
        return jnp.where(odd, other, own), jnp.where(odd, own, other)

    def by_far(own, other):
        return jnp.where(far, other, own), jnp.where(far, own, other)

    def lanes(values, count, size):
        return [
            jnp.where(
                odd,
                values[:, (2 * i + 1) * size : (2 * i + 2) * size],
                values[:, 2 * i * size : (2 * i + 1) * size],
            )
            for i in range(count)
        ]

    halves = tokens.reshape(2, 2, 32, D)
    kept = pick(halves, 1, core)
    got = core_swap(pick(halves, 1, 1 - core))
    quad = jnp.concatenate(by_core(kept, got), 0)
    quad_send = jnp.broadcast_to(quad[:, None], (4, 4, 32, D)).reshape(16, 32, D)
    query_parts = lanes(w_query[0], 4, HD)
    kv_w = jnp.where(odd, w_value[0], w_key[0])
    head_w = jnp.stack(
        [
            jnp.concatenate([query_parts[i], kv_w[:, i * HD : (i + 1) * HD]], 1)
            for i in range(4)
        ]
    )
    head_send = jnp.broadcast_to(fold(head_w)[None], (4, 4, 16, D)).reshape(16, 16, D)
    gain_row = jnp.concatenate([norm_attn[0], norm_mlp[0], norm_query[0], norm_key[0]])
    gain_send = jnp.broadcast_to(jnp.pad(gain_row, (0, D - 144)), (16, 8, D))
    fetched = exchange(jnp.concatenate([quad_send, head_send, gain_send], 1))
    seg_other = core_swap(segments)
    cot_own = cotangent.reshape(128, D)
    cot_both = jnp.concatenate([cot_own, core_swap(cot_own)], 0)

    w_gate, w_up, w_down, w_output, _ = lax.optimization_barrier(
        (w_gate, w_up, w_down, w_output, got)
    )
    out_part = jnp.concatenate(
        [
            jnp.where(
                odd,
                w_output[0, (2 * i + 1) * HD : (2 * i + 2) * HD],
                w_output[0, 2 * i * HD : (2 * i + 1) * HD],
            )
            for i in range(4)
        ],
        0,
    )
    down_part = jnp.where(odd, w_down[0, 768:], w_down[0, :768])
    weights = lax.all_gather(
        jnp.concatenate(
            lanes(w_gate[0], 1, 768) + lanes(w_up[0], 1, 768) + [down_part.T, out_part.T], 1
        ),
        "ctx",
        axis=0,
        tiled=True,
    )
    gateup_w = weights[:, :1536]
    down_wt = weights[:, 1536:2304]
    out_wt = weights[:, 2304:]

    token_half = fetched[:, :32]
    more_half = core_swap(token_half)
    seq_halves = by_core(token_half, more_half)
    seq_tokens = jnp.stack(seq_halves, 1).reshape(1024, D)
    qkv_w = unfold(fetched[:, 32:48]).reshape(1024, 256)
    gains = fetched[:, 48].astype(f32)
    attn_gain = gains[:, :64].reshape(D)
    mlp_gain = gains[:, 64:128].reshape(D)
    qnorm_gain = gains[:, 128:136].reshape(HD)
    knorm_gain = gains[:, 136:144].reshape(HD)

    seg_pair = jnp.where(seq_role // 2 == core, segments, seg_other)
    seg_row = pick(seg_pair, 0, seq_role % 2)
    cosine, sine = rope_tables(seg_row)
    seg_column, seg_row = seg_row[:, None], seg_row[None, :]
    flag = core.reshape(1)
    rope_both = jnp.concatenate([cosine, sine], 1)

    def rope(values):
        turned = jnp.concatenate([values[:, HD // 2 :], values[:, : HD // 2]], -1)
        return values * cosine + turned * sine

    attn_in = (rms_norm(seq_tokens.astype(f32)) * attn_gain).astype(bf16)
    raw = mm(attn_in, qkv_w)
    query_raw, kv_raw = raw[:, :HD], raw[:, HD:]
    queries = rope(rms_norm(query_raw) * qnorm_gain).astype(bf16)
    kv_own = jnp.where(odd, kv_raw, rope(rms_norm(kv_raw) * knorm_gain)).astype(bf16)
    kv_other = core_swap(kv_own)
    mixed_head, lse = kernel_call(
        attend_kernel,
        [shape((1024, HD), bf16), shape((1024, 1), f32)],
        4 * 640 * 1024 * HD,
        flag,
        queries,
        kv_own,
        kv_other,
        seg_column,
        seg_row,
    )
    mixed = exchange(after(mixed_head, cot_both).reshape(16, 64, HD)).reshape(4, 4, 64, HD)
    mixed = jnp.concatenate([mixed[:, i] for i in range(4)], -1).reshape(256, 512)

    def pair_sum(own, other):
        part = (own + core_swap(other.astype(bf16)).astype(f32)).astype(bf16)
        return part.astype(f32) + tp_swap(part).astype(f32)

    mixed_out = mm_nt(mixed, out_wt).reshape(2, 128, D)
    hidden = tokens.reshape(128, D).astype(f32)
    hidden_mid = hidden + pair_sum(pick(mixed_out, 0, core), pick(mixed_out, 0, 1 - core))

    mlp_own = (rms_norm(hidden_mid) * mlp_gain).astype(bf16)
    mlp_in = jnp.concatenate([mlp_own, core_swap(mlp_own)], 0)
    gate_up = mm(mlp_in, gateup_w)
    gate_pre, up_pre = gate_up[:, :768], gate_up[:, 768:]
    sig = jax.nn.sigmoid(gate_pre)
    act = (gate_pre * sig * up_pre).astype(bf16)
    act_grad = mm(cot_both, down_wt)
    gate_grad = (act_grad * up_pre * sig * (1.0 + gate_pre * (1.0 - sig))).astype(bf16)
    up_grad = (act_grad * (gate_pre * sig)).astype(bf16)
    gateup_grad = jnp.concatenate([gate_grad, up_grad], 1)
    mlp_back = mm_nt(gateup_grad, gateup_w)
    mlp_w_grad = kernel_call(
        mlp_grad_kernel,
        [shape((D, 2304), bf16)],
        2 * 256 * 2304 * D,
        (rep // 2).reshape(1),
        mlp_in,
        gateup_grad,
        cot_both,
        act,
    )[0]
    mlp_in_grad = after(pair_sum(mlp_back[:128], mlp_back[128:]), mlp_w_grad)
    mlp_w_grad = lax.psum_scatter(mlp_w_grad, "ctx", scatter_dimension=0, tiled=True)
    mid_back, mlp_gain_grad = norm_back(hidden_mid, mlp_gain, mlp_in_grad)
    grad = cot_own.astype(f32) + mid_back
    grad_own = grad.astype(bf16)
    grad_low = jnp.concatenate(by_core(grad_own, core_swap(grad_own)), 0)
    mixed_grad = kernel_call(
        mixed_grad_kernel,
        [shape((16, 64, HD), bf16)],
        2 * 256 * 512 * D,
        flag,
        grad_low,
        out_wt,
    )[0]
    mixed_grad = exchange(mixed_grad).reshape(1024, HD)
    kv_keep, kv_give, query_low, qgain_grad = kernel_call_scratch(
        attend_back_kernel,
        [
            shape((1024, HD), f32),
            shape((1024, HD), f32),
            shape((1024, HD), bf16),
            shape((1, HD), f32),
        ],
        [pltpu.VMEM((1024, HD), f32), pltpu.VMEM((1024, HD), f32)],
        10 * 640 * 1024 * HD,
        flag,
        queries,
        kv_own,
        kv_other,
        seg_column,
        seg_row,
        lse,
        mixed_grad,
        raw,
        qnorm_gain[None],
        rope_both,
    )
    in_half, in_give, qkv_fold, attn_gain_grad, kgain_grad = kernel_call_scratch(
        project_back_kernel,
        [
            shape((16, 32, D), f32),
            shape((16, 32, D), bf16),
            shape((16, 16, D), bf16),
            shape((1, D), f32),
            shape((1, HD), f32),
        ],
        [pltpu.VMEM((1024, D), bf16)],
        4 * 1024 * 1024 * 256,
        flag,
        kv_keep,
        core_swap(kv_give),
        raw,
        knorm_gain[None],
        rope_both,
        query_low,
        token_half,
        more_half,
        attn_gain[None],
        qkv_w,
    )
    in_pair = in_half + core_swap(in_give).astype(f32)
    gain_grads = jnp.concatenate(
        [
            attn_gain_grad.reshape(16, 64),
            (0.5 * mlp_gain_grad).reshape(16, 64),
            qgain_grad.reshape(16, 8),
            kgain_grad.reshape(16, 8),
        ],
        1,
    ).astype(bf16)
    gain_grads = jnp.pad(gain_grads[:, None], ((0, 0), (0, 7), (0, D - 144)))
    sending = jnp.concatenate([in_pair.astype(bf16), qkv_fold, gain_grads], 1)
    returned = exchange(sending)
    act, grad_low, _ = lax.optimization_barrier((act, grad_low, sending))
    mlp_out = mm_nt(act, down_wt)
    out_tokens = hidden_mid + pair_sum(mlp_out[:128], mlp_out[128:])
    out_w_grad = mm_tn(grad_low, mixed).astype(bf16)
    out_w_grad = exchange(after(out_w_grad, returned).reshape(16, 64, 512))
    returned, mlp_w_grad = lax.optimization_barrier((returned, mlp_w_grad))
    out_w_grad = jnp.sum(out_w_grad.astype(f32), 0).astype(bf16)
    in_sum = jnp.sum(returned[:, :32].reshape(4, 4, 32, D).astype(f32), 1).reshape(128, D)
    gain_sum = jnp.sum(returned[:, 48:].astype(f32), 0)
    in_sum = jnp.concatenate([in_sum, gain_sum, jnp.zeros((8, D), f32)], 0).astype(bf16)
    in_sum = in_sum.astype(f32) + tp_swap(in_sum).astype(f32)
    gain_sum = in_sum[128, :256]
    in_sum = in_sum[:128].reshape(2, 2, 32, D)
    in_own = by_core(pick(in_sum, 0, core), core_swap(pick(in_sum, 0, 1 - core)))
    attn_in_grad = jnp.stack(in_own, 1).reshape(128, D)
    input_back, _ = norm_back(hidden, attn_gain, attn_in_grad)
    tokens_grad = grad + input_back

    def owned(part):
        return part.astype(f32) + zlo_swap(part).astype(f32)

    def both(part):
        return by_core(part, core_swap(part))

    mlp_grads = both(owned(mlp_w_grad))
    out_grads = both(owned(out_w_grad))
    qkv_sum = jnp.sum(unfold(returned[:, 32:48]).reshape(4, 4, 64, 256).astype(f32), 0)
    qkv_grads = both(owned(qkv_sum.astype(bf16)))
    gain_sum = gain_sum + zlo_swap(gain_sum)
    gain_sum = gain_sum + core_swap(gain_sum)

    even_qkv, odd_qkv = qkv_grads
    query_w_grad = [part[i, :, :HD] for i in range(4) for part in qkv_grads]
    out_w_grad = [part.T[i * HD : (i + 1) * HD] for i in range(4) for part in out_grads]
    return (
        out_tokens.reshape(2, 64, D),
        tokens_grad.reshape(2, 64, D),
        jnp.concatenate(query_w_grad, 1)[None],
        jnp.concatenate([even_qkv[i, :, HD:] for i in range(4)], 1)[None],
        jnp.concatenate([odd_qkv[i, :, HD:] for i in range(4)], 1)[None],
        jnp.concatenate(out_w_grad, 0)[None],
        jnp.concatenate([part[:, :768] for part in mlp_grads], 1)[None],
        jnp.concatenate([part[:, 768:1536] for part in mlp_grads], 1)[None],
        jnp.concatenate([part[:, 1536:].T for part in mlp_grads], 0)[None],
        gain_sum[None, :64],
        gain_sum[None, 64:128],
        gain_sum[None, 128:136],
        gain_sum[None, 136:144],
    )


def solution(mesh):
    rows = P(None, "ctx", "tp")
    columns = P(None, "tp", "ctx")
    gain = P(None, "ctx")
    token = P("rep", "ctx", None)
    weight_specs = (rows, rows, rows, columns, rows, rows, columns, gain, gain, gain, gain)
    return jax.shard_map(
        shards,
        mesh=mesh,
        in_specs=(token, token, P("rep", None)) + weight_specs,
        out_specs=(token, token) + weight_specs,
        check_vma=False,
    )
```

```python
import math

import jax
import jax.numpy as jnp
from jax import lax
from jax.experimental import pallas as pl
from jax.experimental.pallas import tpu as pltpu
from jax.sharding import PartitionSpec as P

HD = 128
D = 1024
SCALE = 1.0 / math.sqrt(HD)
norm_eps = 1e-06
rope_base = 1000000.0
masked_score = -1e30
bf16 = jnp.bfloat16
f32 = jnp.float32


def core_swap(values):
    return lax.ppermute(values, "rep", [(0, 1), (1, 0), (2, 3), (3, 2)])


def zlo_swap(values):
    return lax.ppermute(values, "rep", [(0, 2), (1, 3), (2, 0), (3, 1)])


def tp_swap(values):
    return lax.ppermute(values, "tp", [(0, 1), (1, 0)])


def exchange(values):
    return lax.all_to_all(values, "ctx", 0, 0, tiled=True)


def mm(left, right):
    return jnp.dot(left, right, preferred_element_type=f32)


def mm_nt(left, right):
    return lax.dot_general(left, right, (((1,), (1,)), ((), ())), preferred_element_type=f32)


def mm_tn(left, right):
    return lax.dot_general(left, right, (((0,), (0,)), ((), ())), preferred_element_type=f32)


def rms_norm(values):
    return values * lax.rsqrt(jnp.mean(values * values, -1, keepdims=True) + norm_eps)


def norm_back(values, gain, upstream):
    inverse = lax.rsqrt(jnp.mean(values * values, -1, keepdims=True) + norm_eps)
    normed = values * inverse
    scaled = upstream * gain
    value_grad = inverse * (scaled - normed * jnp.mean(scaled * normed, -1, keepdims=True))
    return value_grad, jnp.sum(upstream * normed, 0, keepdims=True)


def rotate(values, cosine, sine):
    return values * cosine + pltpu.roll(values, HD // 2, 1) * sine


def rotate_back(values, cosine, sine):
    return values * cosine - pltpu.roll(values, HD // 2, 1) * sine


def kernel_call(body, out_shape, flops, *operands):
    return kernel_call_scratch(body, out_shape, [], flops, *operands)


def kernel_call_scratch(body, out_shape, scratch, flops, *operands):
    specs = [pl.BlockSpec(memory_space=pltpu.SMEM)]
    specs += [pl.BlockSpec(memory_space=pltpu.VMEM)] * (len(operands) - 1)
    size = sum(math.prod(x.shape) * x.dtype.itemsize for x in list(operands) + list(out_shape))
    return pl.pallas_call(
        body,
        out_shape=out_shape,
        in_specs=specs,
        out_specs=[pl.BlockSpec(memory_space=pltpu.VMEM)] * len(out_shape),
        scratch_shapes=scratch,
        cost_estimate=pl.CostEstimate(flops=flops, bytes_accessed=size, transcendentals=0),
        compiler_params=pltpu.CompilerParams(vmem_limit_bytes=48 << 20),
    )(*operands)


def shape(dims, dtype):
    return jax.ShapeDtypeStruct(dims, dtype)


BLOCK = 256


def masked_scores(queries, keys, seg_column, seg_row, start, length):
    row = start + lax.broadcasted_iota(jnp.int32, (BLOCK, length), 0)
    column = lax.broadcasted_iota(jnp.int32, (BLOCK, length), 1)
    allowed = (seg_column == seg_row) & (column <= row)
    return jnp.where(allowed, mm_nt(queries, keys) * SCALE, masked_score)


def attend_kernel(odd, q_ref, own_ref, other_ref, segc_ref, segr_ref, mixed_ref, lse_ref):
    own, other = own_ref[...], other_ref[...]
    flag = odd[0] == 1
    keys, values = jnp.where(flag, other, own), jnp.where(flag, own, other)
    for start in range(0, 1024, BLOCK):
        rows = slice(start, start + BLOCK)
        length = start + BLOCK
        scores = masked_scores(
            q_ref[rows], keys[:length], segc_ref[rows], segr_ref[:, :length], start, length
        )
        row_max = jnp.max(scores, -1, keepdims=True)
        weights_exp = jnp.exp(scores - row_max)
        row_total = jnp.sum(weights_exp, -1, keepdims=True)
        probs = (weights_exp * (1.0 / row_total)).astype(bf16)
        mixed_ref[rows] = mm(probs, values[:length]).astype(bf16)
        lse_ref[rows] = row_max + jnp.log(row_total)


def attend_back_kernel(
    odd,
    q_ref,
    own_ref,
    other_ref,
    segc_ref,
    segr_ref,
    lse_ref,
    up_ref,
    raw_ref,
    gain_ref,
    rope_ref,
    keep_ref,
    give_ref,
    low_ref,
    gain_grad_ref,
    key_sum,
    value_sum,
):
    own, other = own_ref[...], other_ref[...]
    flag = odd[0] == 1
    keys, values = jnp.where(flag, other, own), jnp.where(flag, own, other)
    gain_grad = jnp.zeros((1, HD), f32)
    for start in range(1024 - BLOCK, -1, -BLOCK):
        rows = slice(start, start + BLOCK)
        length = start + BLOCK
        queries, upstream = q_ref[rows], up_ref[rows]
        scores = masked_scores(
            queries, keys[:length], segc_ref[rows], segr_ref[:, :length], start, length
        )
        probs = jnp.exp(scores - lse_ref[rows])
        value_part = mm_tn(probs.astype(bf16), upstream)
        prob_grad = mm_nt(upstream, values[:length])
        score_grad = (
            probs * (prob_grad - jnp.sum(probs * prob_grad, -1, keepdims=True))
        ).astype(bf16)
        key_part = mm_tn(score_grad, queries)
        if length == 1024:
            value_sum[...] = value_part
            key_sum[...] = key_part
        else:
            value_sum[:length] += value_part
            key_sum[:length] += key_part
        query_grad = mm(score_grad, keys[:length]) * SCALE
        back, part = norm_back(
            raw_ref[rows, :HD],
            gain_ref[...],
            rotate_back(query_grad, rope_ref[rows, :HD], rope_ref[rows, HD:]),
        )
        low_ref[rows] = back.astype(bf16)
        gain_grad += part
    gain_grad_ref[...] = gain_grad
    key_grad, value_grad = key_sum[...] * SCALE, value_sum[...]
    keep_ref[...] = jnp.where(flag, value_grad, key_grad)
    give_ref[...] = jnp.where(flag, key_grad, value_grad)


def project_back_kernel(
    odd,
    keep_ref,
    got_ref,
    raw_ref,
    gain_ref,
    rope_ref,
    low_ref,
    tokens_ref,
    more_tokens_ref,
    token_gain_ref,
    w_ref,
    half_ref,
    give_ref,
    fold_ref,
    attn_gain_ref,
    gain_grad_ref,
    attn_in,
):
    flag = odd[0] == 1
    total = keep_ref[...] + got_ref[...]
    back, part = norm_back(
        raw_ref[:, HD:],
        gain_ref[...],
        rotate_back(total, rope_ref[:, :HD], rope_ref[:, HD:]),
    )
    gain_grad_ref[...] = jnp.where(flag, 0.0, part)
    raw_grad = jnp.concatenate([low_ref[...], jnp.where(flag, total, back).astype(bf16)], 1)
    attn_gain = jnp.zeros((1, D), f32)
    for start in range(0, 1024, BLOCK):
        rows = slice(start, start + BLOCK)
        blocks = slice(start // 64, (start + BLOCK) // 64)
        in_part = mm_nt(raw_grad[rows], w_ref[...])
        held, more = tokens_ref[blocks], more_tokens_ref[blocks]
        tokens = jnp.stack([jnp.where(flag, more, held), jnp.where(flag, held, more)], 1)
        normed = rms_norm(tokens.reshape(BLOCK, D).astype(f32))
        attn_in[rows] = (normed * token_gain_ref[...]).astype(bf16)
        attn_gain += jnp.sum(in_part * normed, 0, keepdims=True)
        halves = in_part.reshape(4, 2, 32, D)
        half_ref[blocks] = jnp.where(flag, halves[:, 1], halves[:, 0])
        give_ref[blocks] = jnp.where(flag, halves[:, 0], halves[:, 1]).astype(bf16)
    for start in range(0, D, BLOCK):
        rows = slice(start, start + BLOCK)
        blocks = slice(start // 64, (start + BLOCK) // 64)
        w_grad = mm_tn(attn_in[:, rows], raw_grad).astype(bf16).reshape(4, 4, 16, 256)
        for i in range(4):
            fold_ref[blocks, :, 256 * i : 256 * i + 256] = w_grad[:, i]
    attn_gain_ref[...] = attn_gain


def mlp_grad_kernel(unused, in_ref, up_ref, cot_ref, act_ref, out_ref):
    for start in range(0, D, BLOCK):
        rows = slice(start, start + BLOCK)
        out_ref[rows, :1536] = mm_tn(in_ref[:, rows], up_ref[...]).astype(bf16)
        out_ref[rows, 1536:] = mm_tn(cot_ref[:, rows], act_ref[...]).astype(bf16)


def mixed_grad_kernel(unused, grad_ref, w_ref, out_ref):
    out = mm(grad_ref[...], w_ref[...]).astype(bf16)
    for i in range(4):
        for j in range(4):
            out_ref[4 * i + j] = out[64 * i : 64 * i + 64, HD * j : HD * j + HD]


def rope_tables(seg_row):
    length = seg_row.shape[0]
    starts = jnp.zeros((length,), jnp.int32)
    for doc in range(1, 4):
        before = jnp.sum((seg_row < doc).astype(jnp.int32))
        starts = jnp.where(seg_row == doc, before, starts)
    pos = jnp.arange(length, dtype=jnp.int32) - starts
    half_size = HD // 2
    freq_table = jnp.exp(
        jnp.arange(half_size, dtype=f32) * (-2.0 * math.log(rope_base) / HD)
    )
    angles = pos.astype(f32)[:, None] * freq_table
    cosine, sine = jnp.cos(angles), jnp.sin(angles)
    return jnp.concatenate([cosine, cosine], -1), jnp.concatenate([-sine, sine], -1)


def after(values, *others):
    return lax.optimization_barrier((values,) + others)[0]


def fold(rows):
    count = rows.shape[0]
    parts = rows.reshape(count, 4, 16, 256)
    return jnp.concatenate([parts[:, i] for i in range(4)], -1)


def unfold(rows):
    count = rows.shape[0]
    return jnp.stack([rows[:, :, 256 * i : 256 * i + 256] for i in range(4)], 1).reshape(
        count, 64, 256
    )


def shards(
    tokens,
    cotangent,
    segments,
    w_query,
    w_key,
    w_value,
    w_output,
    w_gate,
    w_up,
    w_down,
    norm_attn,
    norm_mlp,
    norm_query,
    norm_key,
):
    rep = lax.axis_index("rep")
    core = rep % 2
    odd = core == 1
    far = rep // 2 == 1
    ctx = lax.axis_index("ctx")
    seq_role = ctx // 4

    def pick(values, axis, index):
        return lax.dynamic_index_in_dim(values, index, axis, keepdims=False)

    def by_core(own, other):
        return jnp.where(odd, other, own), jnp.where(odd, own, other)

    def by_far(own, other):
        return jnp.where(far, other, own), jnp.where(far, own, other)

    def lanes(values, count, size):
        return [
            jnp.where(
                odd,
                values[:, (2 * i + 1) * size : (2 * i + 2) * size],
                values[:, 2 * i * size : (2 * i + 1) * size],
            )
            for i in range(count)
        ]

    halves = tokens.reshape(2, 2, 32, D)
    kept = pick(halves, 1, core)
    got = core_swap(pick(halves, 1, 1 - core))
    quad = jnp.concatenate(by_core(kept, got), 0)
    quad_send = jnp.broadcast_to(quad[:, None], (4, 4, 32, D)).reshape(16, 32, D)
    query_parts = lanes(w_query[0], 4, HD)
    kv_w = jnp.where(odd, w_value[0], w_key[0])
    head_w = jnp.stack(
        [
            jnp.concatenate([query_parts[i], kv_w[:, i * HD : (i + 1) * HD]], 1)
            for i in range(4)
        ]
    )
    head_send = jnp.broadcast_to(fold(head_w)[None], (4, 4, 16, D)).reshape(16, 16, D)
    gain_row = jnp.concatenate([norm_attn[0], norm_mlp[0], norm_query[0], norm_key[0]])
    gain_send = jnp.broadcast_to(jnp.pad(gain_row, (0, D - 144)), (16, 8, D))
    fetched = exchange(jnp.concatenate([quad_send, head_send, gain_send], 1))
    seg_other = core_swap(segments)
    cot_own = cotangent.reshape(128, D)
    cot_both = jnp.concatenate([cot_own, core_swap(cot_own)], 0)

    w_gate, w_up, w_down, w_output, _ = lax.optimization_barrier(
        (w_gate, w_up, w_down, w_output, got)
    )
    out_part = jnp.concatenate(
        [
            jnp.where(
                odd,
                w_output[0, (2 * i + 1) * HD : (2 * i + 2) * HD],
                w_output[0, 2 * i * HD : (2 * i + 1) * HD],
            )
            for i in range(4)
        ],
        0,
    )
    down_part = jnp.where(odd, w_down[0, 768:], w_down[0, :768])
    weights = lax.all_gather(
        jnp.concatenate(
            lanes(w_gate[0], 1, 768) + lanes(w_up[0], 1, 768) + [down_part.T, out_part.T], 1
        ),
        "ctx",
        axis=0,
        tiled=True,
    )
    gateup_w = weights[:, :1536]
    down_wt = weights[:, 1536:2304]
    out_wt = weights[:, 2304:]

    token_half = fetched[:, :32]
    more_half = core_swap(token_half)
    seq_halves = by_core(token_half, more_half)
    seq_tokens = jnp.stack(seq_halves, 1).reshape(1024, D)
    qkv_w = unfold(fetched[:, 32:48]).reshape(1024, 256)
    gains = fetched[:, 48].astype(f32)
    attn_gain = gains[:, :64].reshape(D)
    mlp_gain = gains[:, 64:128].reshape(D)
    qnorm_gain = gains[:, 128:136].reshape(HD)
    knorm_gain = gains[:, 136:144].reshape(HD)

    seg_pair = jnp.where(seq_role // 2 == core, segments, seg_other)
    seg_row = pick(seg_pair, 0, seq_role % 2)
    cosine, sine = rope_tables(seg_row)
    seg_column, seg_row = seg_row[:, None], seg_row[None, :]
    flag = core.reshape(1)
    rope_both = jnp.concatenate([cosine, sine], 1)

    def rope(values):
        turned = jnp.concatenate([values[:, HD // 2 :], values[:, : HD // 2]], -1)
        return values * cosine + turned * sine

    attn_in = (rms_norm(seq_tokens.astype(f32)) * attn_gain).astype(bf16)
    raw = mm(attn_in, qkv_w)
    query_raw, kv_raw = raw[:, :HD], raw[:, HD:]
    queries = rope(rms_norm(query_raw) * qnorm_gain).astype(bf16)
    kv_own = jnp.where(odd, kv_raw, rope(rms_norm(kv_raw) * knorm_gain)).astype(bf16)
    kv_other = core_swap(kv_own)
    mixed_head, lse = kernel_call(
        attend_kernel,
        [shape((1024, HD), bf16), shape((1024, 1), f32)],
        4 * 640 * 1024 * HD,
        flag,
        queries,
        kv_own,
        kv_other,
        seg_column,
        seg_row,
    )
    mixed = exchange(after(mixed_head, cot_both).reshape(16, 64, HD)).reshape(4, 4, 64, HD)
    mixed = jnp.concatenate([mixed[:, i] for i in range(4)], -1).reshape(256, 512)

    def pair_sum(own, other):
        part = (own + core_swap(other.astype(bf16)).astype(f32)).astype(bf16)
        return part.astype(f32) + tp_swap(part).astype(f32)

    mixed_out = mm_nt(mixed, out_wt).reshape(2, 128, D)
    hidden = tokens.reshape(128, D).astype(f32)
    hidden_mid = hidden + pair_sum(pick(mixed_out, 0, core), pick(mixed_out, 0, 1 - core))

    mlp_own = (rms_norm(hidden_mid) * mlp_gain).astype(bf16)
    mlp_in = jnp.concatenate([mlp_own, core_swap(mlp_own)], 0)
    gate_up = mm(mlp_in, gateup_w)
    gate_pre, up_pre = gate_up[:, :768], gate_up[:, 768:]
    sig = jax.nn.sigmoid(gate_pre)
    act = (gate_pre * sig * up_pre).astype(bf16)
    act_grad = mm(cot_both, down_wt)
    gate_grad = (act_grad * up_pre * sig * (1.0 + gate_pre * (1.0 - sig))).astype(bf16)
    up_grad = (act_grad * (gate_pre * sig)).astype(bf16)
    gateup_grad = jnp.concatenate([gate_grad, up_grad], 1)
    mlp_back = mm_nt(gateup_grad, gateup_w)
    mlp_w_grad = kernel_call(
        mlp_grad_kernel,
        [shape((D, 2304), bf16)],
        2 * 256 * 2304 * D,
        (rep // 2).reshape(1),
        mlp_in,
        gateup_grad,
        cot_both,
        act,
    )[0]
    mlp_in_grad = after(pair_sum(mlp_back[:128], mlp_back[128:]), mlp_w_grad)
    mlp_w_grad = lax.psum_scatter(mlp_w_grad, "ctx", scatter_dimension=0, tiled=True)
    mid_back, mlp_gain_grad = norm_back(hidden_mid, mlp_gain, mlp_in_grad)
    grad = cot_own.astype(f32) + mid_back
    grad_own = grad.astype(bf16)
    grad_low = jnp.concatenate(by_core(grad_own, core_swap(grad_own)), 0)
    mixed_grad = kernel_call(
        mixed_grad_kernel,
        [shape((16, 64, HD), bf16)],
        2 * 256 * 512 * D,
        flag,
        grad_low,
        out_wt,
    )[0]
    mixed_grad = exchange(mixed_grad).reshape(1024, HD)
    kv_keep, kv_give, query_low, qgain_grad = kernel_call_scratch(
        attend_back_kernel,
        [
            shape((1024, HD), f32),
            shape((1024, HD), f32),
            shape((1024, HD), bf16),
            shape((1, HD), f32),
        ],
        [pltpu.VMEM((1024, HD), f32), pltpu.VMEM((1024, HD), f32)],
        10 * 640 * 1024 * HD,
        flag,
        queries,
        kv_own,
        kv_other,
        seg_column,
        seg_row,
        lse,
        mixed_grad,
        raw,
        qnorm_gain[None],
        rope_both,
    )
    in_half, in_give, qkv_fold, attn_gain_grad, kgain_grad = kernel_call_scratch(
        project_back_kernel,
        [
            shape((16, 32, D), f32),
            shape((16, 32, D), bf16),
            shape((16, 16, D), bf16),
            shape((1, D), f32),
            shape((1, HD), f32),
        ],
        [pltpu.VMEM((1024, D), bf16)],
        4 * 1024 * 1024 * 256,
        flag,
        kv_keep,
        core_swap(kv_give),
        raw,
        knorm_gain[None],
        rope_both,
        query_low,
        token_half,
        more_half,
        attn_gain[None],
        qkv_w,
    )
    in_pair = in_half + core_swap(in_give).astype(f32)
    gain_grads = jnp.concatenate(
        [
            attn_gain_grad.reshape(16, 64),
            (0.5 * mlp_gain_grad).reshape(16, 64),
            qgain_grad.reshape(16, 8),
            kgain_grad.reshape(16, 8),
        ],
        1,
    ).astype(bf16)
    gain_grads = jnp.pad(gain_grads[:, None], ((0, 0), (0, 7), (0, D - 144)))
    sending = jnp.concatenate([in_pair.astype(bf16), qkv_fold, gain_grads], 1)
    returned = exchange(sending)
    act, grad_low, _ = lax.optimization_barrier((act, grad_low, sending))
    mlp_out = mm_nt(act, down_wt)
    out_tokens = hidden_mid + pair_sum(mlp_out[:128], mlp_out[128:])
    out_w_grad = mm_tn(grad_low, mixed).astype(bf16)
    returned, mlp_w_grad, out_w_grad, _ = lax.optimization_barrier(
        (returned, mlp_w_grad, out_w_grad, out_tokens)
    )
    out_w_grad = exchange(out_w_grad.reshape(16, 64, 512))
    out_w_grad = jnp.sum(out_w_grad.astype(f32), 0).astype(bf16)
    in_sum = jnp.sum(returned[:, :32].reshape(4, 4, 32, D).astype(f32), 1).reshape(128, D)
    gain_sum = jnp.sum(returned[:, 48:].astype(f32), 0)
    in_sum = jnp.concatenate([in_sum, gain_sum, jnp.zeros((8, D), f32)], 0).astype(bf16)
    in_sum = in_sum.astype(f32) + tp_swap(in_sum).astype(f32)
    gain_sum = in_sum[128, :256]
    in_sum = in_sum[:128].reshape(2, 2, 32, D)
    in_own = by_core(pick(in_sum, 0, core), core_swap(pick(in_sum, 0, 1 - core)))
    attn_in_grad = jnp.stack(in_own, 1).reshape(128, D)
    input_back, _ = norm_back(hidden, attn_gain, attn_in_grad)
    tokens_grad = grad + input_back

    def owned(part):
        return part.astype(f32) + zlo_swap(part).astype(f32)

    def both(part):
        return by_core(part, core_swap(part))

    mlp_grads = both(owned(mlp_w_grad))
    out_grads = both(owned(out_w_grad))
    qkv_sum = jnp.sum(unfold(returned[:, 32:48]).reshape(4, 4, 64, 256).astype(f32), 0)
    qkv_grads = both(owned(qkv_sum.astype(bf16)))
    gain_sum = gain_sum + zlo_swap(gain_sum)
    gain_sum = gain_sum + core_swap(gain_sum)

    even_qkv, odd_qkv = qkv_grads
    query_w_grad = [part[i, :, :HD] for i in range(4) for part in qkv_grads]
    out_w_grad = [part.T[i * HD : (i + 1) * HD] for i in range(4) for part in out_grads]
    return (
        out_tokens.reshape(2, 64, D),
        tokens_grad.reshape(2, 64, D),
        jnp.concatenate(query_w_grad, 1)[None],
        jnp.concatenate([even_qkv[i, :, HD:] for i in range(4)], 1)[None],
        jnp.concatenate([odd_qkv[i, :, HD:] for i in range(4)], 1)[None],
        jnp.concatenate(out_w_grad, 0)[None],
        jnp.concatenate([part[:, :768] for part in mlp_grads], 1)[None],
        jnp.concatenate([part[:, 768:1536] for part in mlp_grads], 1)[None],
        jnp.concatenate([part[:, 1536:].T for part in mlp_grads], 0)[None],
        gain_sum[None, :64],
        gain_sum[None, 64:128],
        gain_sum[None, 128:136],
        gain_sum[None, 136:144],
    )


def solution(mesh):
    rows = P(None, "ctx", "tp")
    columns = P(None, "tp", "ctx")
    gain = P(None, "ctx")
    token = P("rep", "ctx", None)
    weight_specs = (rows, rows, rows, columns, rows, rows, columns, gain, gain, gain, gain)
    return jax.shard_map(
        shards,
        mesh=mesh,
        in_specs=(token, token, P("rep", None)) + weight_specs,
        out_specs=(token, token) + weight_specs,
        check_vma=False,
    )
```
